512 devices in a mesh: blk: 512 (over y, x, z, core).
Axes of the slice: x: 4, y: 8, z: 8, core: 2. Of those that a mesh axis runs over, the one named last changes fastest.
Arguments:
- pair_density: bfloat16 [196608, 2048], P('blk'), may hold values from -6 to 6
- table: int32 [3, 196608], P(None, 'blk'), may hold values from 0 to 4095, as said below
- gvec: int32 [3, 2048], replicated, may hold values from -8 to 8
- val_energy: float32 [4096, 4], replicated, may hold values from -8 to -0.5
- cond_energy: float32 [4096, 8], replicated, may hold values from 0.5 to 8
Outputs:
- kernel_band: float32 [196608, 1920], P('blk')
The draws below stay inside these ranges and needn't reach their ends.
Inputs may be any that keep to these rules, and one draw needn't show every extreme that they name: table[0] holds valence bands below 4, table[1] conduction bands below 8, table[2] k-points below 4096.
All inputs are finite; a program needn't handle non-finite values.
Results may differ from the reference program's by a relative error of at most 0.0037.
Values may be sent and summed in bfloat16 or wider, within the bound.
A program may use at most 64 MiB of HBM per device.

```python
import jax
import jax.numpy as jnp
from jax import lax

NG = 2048
NV = 4
NC = 8
NK = 4096
TR_DEV = 384
TRANS = 196608
N_BLK = 512


def draw_table(key, part):
    key = jax.random.fold_in(key, 7)
    first, second, third = jax.random.split(key, 3)
    valence = jax.random.randint(first, (TRANS,), 0, NV)
    conduction = jax.random.randint(second, (TRANS,), 0, NC)
    kpoint = jax.random.randint(third, (TRANS,), 0, NK)
    position = jnp.arange(TRANS)
    valence = jnp.where(position == 0, NV - 1, jnp.where(position == 1, 0, valence))
    conduction = jnp.where(position == 0, NC - 1, conduction)
    kpoint = jnp.where(position == 0, NK - 1, kpoint)
    return jnp.stack([valence, conduction, kpoint]).astype(jnp.int32)


def with_ends(values, own_key, low, largest):
    extent = values.shape
    place = [jax.random.randint(jax.random.fold_in(own_key, axis), (), 0, extent[axis]) for axis in range(len(extent))]
    values = values.at[tuple(place)].set(low)
    longest = extent.index(max(extent))
    place[longest] = (place[longest] + 1) % extent[longest]
    return values.at[tuple(place)].set(largest)


def block_scale(key, shape, cuts, smallest, high):
    level = 1.0
    for axis_at, parts in cuts:
        draws = jax.random.uniform(jax.random.fold_in(jax.random.fold_in(key, 6), axis_at), (parts,), jnp.float32, smallest / len(cuts), high / len(cuts))
        level = level * jnp.repeat(jnp.exp(draws), shape[axis_at] // parts).reshape((-1,) + (1,) * (len(shape) - 1 - axis_at))
    return level


def noise(key, shape, scale, bound, pieces=(), held_as=jnp.bfloat16):
    result = jax.random.normal(key, shape, jnp.float32) * scale
    if len(pieces) > 0:
        result = block_scale(key, shape, pieces, -0.22, 0.18) * result
    return jnp.clip(result, min=-bound, max=bound).astype(held_as)


def setup_inputs(seed: int = 0) -> dict:
    key_list = jax.random.split(jax.random.key(seed), 6)
    pair_density = noise(key_list[0], (TRANS, NG), 1.0, 6.0, ((0, 512),))
    table = draw_table(jax.random.fold_in(key_list[5], 71), 0)
    gvec = with_ends(jax.random.randint(key_list[2], (3, NG), -8, 9), jax.random.fold_in(key_list[2], 1), -8, 8).astype(jnp.int32)
    val_energy = jnp.clip(jax.random.uniform(key_list[3], (NK, NV), jnp.float32, -8.0, -0.5), -8.0, -0.5)
    cond_energy = jnp.clip(jax.random.uniform(key_list[4], (NK, NC), jnp.float32, 0.5, 8.0), 0.5, 8.0)
    return {"pair_density": pair_density, "table": table, "gvec": gvec, "val_energy": val_energy, "cond_energy": cond_energy}


def weighting(gvec):
    shifted = gvec.astype(jnp.float32) + jnp.array([0.1, 0.2, 0.3], jnp.float32)[:, None]
    weight = 1.0 / lax.optimization_barrier(jnp.sum(shifted * shifted, axis=0))
    return weight / jnp.mean(weight)

def reference(pair_density, table, gvec, val_energy, cond_energy):
    norm_weight = weighting(gvec)
    scaled = (pair_density.astype(jnp.float32) * jnp.sqrt(norm_weight)[None, :]).astype(jnp.bfloat16)
    energy = cond_energy[table[2], table[1]] - val_energy[table[2], table[0]]
    blocks = scaled.reshape(N_BLK, TR_DEV, NG)
    energies = energy.reshape(N_BLK, TR_DEV)
    factor = 2.0 / jnp.sqrt(jnp.float32(NG))
    eye_mask = jnp.eye(TR_DEV, dtype=jnp.float32)

    def one_block(index):
        mine = blocks[index]
        tiles = []
        for offset in range(-2, 3):
            other = blocks[(index + offset) % N_BLK]
            tile = factor * jnp.dot(mine, other.T, preferred_element_type=jnp.float32)
            if offset == 0:
                tile = tile + eye_mask * energies[index][:, None]
            tiles.append(tile)
        return jnp.concatenate(tiles, axis=1)
    band = lax.map(one_block, jnp.arange(N_BLK, dtype=jnp.int32))
    return band.reshape(TRANS, 5 * TR_DEV)
```

```python
import functools

import jax
import jax.numpy as jnp
from jax import lax
from jax.experimental import pallas as pl
from jax.experimental.pallas import tpu as pltpu
from jax.sharding import PartitionSpec as P

MESH = pl.DeviceIdType.MESH
CHUNK = 128
KSTEP = 512
SCALE_ROWS = 32


def times_transposed(left, right):
    return lax.dot_general(
        left, right, (((1,), (1,)), ((), ())), preferred_element_type=jnp.float32
    )


def picked(values, matches):
    high = values.astype(jnp.bfloat16)
    rest = values - high.astype(jnp.float32)
    middle = rest.astype(jnp.bfloat16)
    low = (rest - middle.astype(jnp.float32)).astype(jnp.bfloat16)
    dot = functools.partial(jnp.dot, preferred_element_type=jnp.float32)
    return dot(high, matches) + dot(middle, matches) + dot(low, matches)


def kernel(
    n, x_ref, table_ref, gvec_ref, val_ref, cond_ref, out_ref,
    both, other, far, far_out, far_in, table, gvec, val, cond, weight, energy,
    local_sem, sib_sem, block_sem, side_sem, back_sem,
):
    rows, width = x_ref.shape
    chunks = rows // CHUNK
    me = lax.axis_index("blk")
    core = lax.rem(me, 2)
    sib = me + 1 - 2 * core
    out = lax.rem(me + n - 1 + 2 * core, n)
    at_own = 2 * rows
    at_sib = pl.multiple_of((3 - 2 * core) * rows, 128)
    at_out = pl.multiple_of((1 + 2 * core) * rows, 128)
    at_far = pl.multiple_of((4 * core) * rows, 128)
    at_side = pl.multiple_of((4 * core) * rows, 128)

    def remote(src, dst, sems, i, device):
        return pltpu.make_async_remote_copy(
            src_ref=src, dst_ref=dst, send_sem=sems.at[0, i], recv_sem=sems.at[1, i],
            device_id=(device,), device_id_type=MESH,
        )

    barrier = pltpu.get_barrier_semaphore()
    for peer in (out, sib):
        pl.semaphore_signal(barrier, inc=1, device_id=(peer,), device_id_type=MESH)

    locals_ = [
        pltpu.make_async_copy(src, dst, local_sem.at[i])
        for i, (src, dst) in enumerate(
            [
                (gvec_ref, gvec),
                (x_ref, both.at[pl.ds(0, rows)]),
                (table_ref, table),
                (val_ref, val),
                (cond_ref, cond),
            ]
        )
    ]
    for copy in locals_:
        copy.start()
    pl.semaphore_wait(barrier, 2)

    blocks = []
    for i in range(chunks):
        part = pl.ds(i * CHUNK, CHUNK)
        blocks.append(remote(x_ref.at[part], other.at[part], block_sem, i, out))
        blocks[-1].start()
    beside = remote(x_ref, both.at[pl.ds(rows, rows)], sib_sem, 0, sib)
    beside.start()

    locals_[0].wait()
    total = jnp.zeros((1, width), jnp.float32)
    for axis, shift in enumerate((0.1, 0.2, 0.3)):
        component = gvec[axis : axis + 1, :].astype(jnp.float32) + jnp.float32(shift)
        total = total + component * component
    inverse = 1.0 / total
    weight[...] = jnp.sqrt(inverse / jnp.mean(inverse))

    def scale(ref, first, count):
        def body(step, carry):
            part = pl.ds(pl.multiple_of(first + step * SCALE_ROWS, SCALE_ROWS), SCALE_ROWS)
            ref[part, :] = (ref[part, :].astype(jnp.float32) * weight[...]).astype(jnp.bfloat16)
            return carry

        lax.fori_loop(0, count // SCALE_ROWS, body, 0)

    factor = 2.0 / jnp.sqrt(jnp.full((1, 1), width, jnp.float32))

    for copy in locals_[2:]:
        copy.wait()
    nk = cond.shape[1]
    k_row = table[2:3, :]

    def match(step, carry):
        of_val, of_cond = carry
        first = pl.multiple_of(step * KSTEP, KSTEP)
        numbers = lax.broadcasted_iota(jnp.int32, (KSTEP, rows), 0) + first
        matches = (numbers == k_row).astype(jnp.float32).astype(jnp.bfloat16)
        part = pl.ds(first, KSTEP)
        return of_val + picked(val[:, part], matches), of_cond + picked(cond[:, part], matches)

    of_val, of_cond = lax.fori_loop(
        0, nk // KSTEP, match,
        (jnp.zeros((val.shape[0], rows), jnp.float32), jnp.zeros((cond.shape[0], rows), jnp.float32)),
    )

    def band(values, chosen):
        bands = lax.broadcasted_iota(jnp.int32, values.shape, 0)
        return jnp.sum(jnp.where(bands == chosen, values, 0.0), axis=0, keepdims=True)

    energy[...] = band(of_cond, table[1:2, :]) - band(of_val, table[0:1, :])

    locals_[1].wait()
    scale(both, 0, rows)

    def own(step, carry):
        first = pl.multiple_of(step * CHUNK, CHUNK)
        part = pl.ds(first, CHUNK)
        tile = factor * times_transposed(both[part, :], both[pl.ds(0, rows), :])
        i = lax.broadcasted_iota(jnp.int32, tile.shape, 0) + first
        j = lax.broadcasted_iota(jnp.int32, tile.shape, 1)
        out_ref[part, pl.ds(at_own, rows)] = tile + jnp.where(i == j, energy[...], 0.0)
        return carry

    lax.fori_loop(0, chunks, own, 0)

    beside.wait_recv()
    scale(both, rows, rows)

    def near(step, carry):
        part = pl.ds(pl.multiple_of(step * CHUNK, CHUNK), CHUNK)
        out_ref[part, pl.ds(at_sib, rows)] = factor * times_transposed(
            both[part, :], both[pl.ds(rows, rows), :]
        )
        return carry

    lax.fori_loop(0, chunks, near, 0)

    sides, backs = [], []
    for i in range(chunks):
        first = i * CHUNK
        part = pl.ds(first, CHUNK)
        blocks[i].wait_recv()
        scale(other, first, CHUNK)
        far_out[part, :] = (
            factor * times_transposed(other[part, :], both[pl.ds(rows, rows), :])
        ).astype(jnp.bfloat16)
        backs.append(remote(far_out.at[part], far_in.at[part], back_sem, i, out))
        backs[-1].start()
        far[i] = factor * times_transposed(both[pl.ds(rows, rows), :], other[part, :])
        sides.append(
            remote(
                far.at[i],
                out_ref.at[:, pl.ds(pl.multiple_of(at_side + first, 128), CHUNK)],
                side_sem, i, sib,
            )
        )
        sides[-1].start()
        out_ref[:, pl.ds(pl.multiple_of(at_out + first, 128), CHUNK)] = factor * times_transposed(
            both[pl.ds(0, rows), :], other[part, :]
        )

    for i in range(chunks):
        part = pl.ds(i * CHUNK, CHUNK)
        backs[i].wait_recv()
        out_ref[part, pl.ds(at_far, rows)] = far_in[part, :].astype(jnp.float32)
    for copy in sides:
        copy.wait()
    for copy in blocks + backs + [beside]:
        copy.wait_send()


def shards(pair_density, table, gvec, val_energy, cond_energy):
    rows, width = pair_density.shape
    n = lax.axis_size("blk")
    nk, nv = val_energy.shape
    nc = cond_energy.shape[1]
    chunks = rows // CHUNK
    anywhere = pl.BlockSpec(memory_space=pltpu.HBM)
    return pl.pallas_call(
        functools.partial(kernel, n),
        out_shape=jax.ShapeDtypeStruct((rows, 5 * rows), jnp.float32),
        in_specs=[anywhere] * 5,
        out_specs=pl.BlockSpec(memory_space=pltpu.VMEM),
        scratch_shapes=[
            pltpu.VMEM((2 * rows, width), jnp.bfloat16),
            pltpu.VMEM((rows, width), jnp.bfloat16),
            pltpu.VMEM((chunks, rows, CHUNK), jnp.float32),
            pltpu.VMEM((rows, rows), jnp.bfloat16),
            pltpu.VMEM((rows, rows), jnp.bfloat16),
            pltpu.VMEM((3, rows), jnp.int32),
            pltpu.VMEM((3, width), jnp.int32),
            pltpu.VMEM((nv, nk), jnp.float32),
            pltpu.VMEM((nc, nk), jnp.float32),
            pltpu.VMEM((1, width), jnp.float32),
            pltpu.VMEM((1, rows), jnp.float32),
            pltpu.SemaphoreType.DMA((5,)),
            pltpu.SemaphoreType.DMA((2, 1)),
            pltpu.SemaphoreType.DMA((2, chunks)),
            pltpu.SemaphoreType.DMA((2, chunks)),
            pltpu.SemaphoreType.DMA((2, chunks)),
        ],
        compiler_params=pltpu.CompilerParams(
            collective_id=0, has_side_effects=True, vmem_limit_bytes=32 << 20
        ),
        name="band",
    )(*[pltpu.with_memory_space_constraint(v, pltpu.HBM) for v in (pair_density, table, gvec, val_energy.T, cond_energy.T)])


def solution(mesh):
    return jax.shard_map(
        shards,
        mesh=mesh,
        in_specs=(P("blk", None), P(None, "blk"), P(), P(), P()),
        out_specs=P("blk", None),
        check_vma=False,
    )
```

```python
import functools

import jax
import jax.numpy as jnp
from jax import lax
from jax.experimental import pallas as pl
from jax.experimental.pallas import tpu as pltpu
from jax.sharding import PartitionSpec as P

MESH = pl.DeviceIdType.MESH
CHUNK = 128
PIECES = (64, 64, 64, 64, 64, 32, 32)
FOOT_WAITS = 3
COLUMN = 8
KSTEP = 512
SCALE_ROWS = 32


def times_transposed(left, right):
    return lax.dot_general(
        left, right, (((1,), (1,)), ((), ())), preferred_element_type=jnp.float32
    )


def in_three(values):
    high = values.astype(jnp.bfloat16).astype(jnp.float32)
    rest = values - high
    middle = rest.astype(jnp.bfloat16).astype(jnp.float32)
    return [high, middle, rest - middle]


def kernel(
    n, x_ref, table_ref, gvec_ref, val_ref, cond_ref, out_ref,
    both, other, relay, far, far_out, far_in, table, gvec, val, cond, terms, weight, energy,
    local_sem, sib_sem, block_sem, relay_sem, side_sem, back_sem, helper_ready, foot_ready,
):
    rows, width = x_ref.shape
    chunks = rows // CHUNK
    parts, first = [], 0
    for size in PIECES:
        parts.append(pl.ds(first, size))
        first += size
    me = lax.axis_index("blk")
    core = lax.rem(me, 2)
    level = lax.rem(me // 2, COLUMN)
    sib = me + 1 - 2 * core
    out = lax.rem(me + n - 1 + 2 * core, n)
    foot = jnp.logical_and(level == 0, core == 0)
    helper = jnp.logical_and(level == 0, core == 1)
    top = jnp.logical_and(level == COLUMN - 1, core == 1)
    my_helper = lax.rem(me + n - 2 * COLUMN + 1, n)
    helped_foot = lax.rem(me + 2 * COLUMN - 1, n)
    helped_top = lax.rem(me + 2 * COLUMN - 2, n)
    top_helper = lax.rem(me + n - 2 * COLUMN + 2, n)
    at_own = 2 * rows
    at_sib = pl.multiple_of((3 - 2 * core) * rows, 128)
    at_out = pl.multiple_of((1 + 2 * core) * rows, 128)
    at_far = pl.multiple_of((4 * core) * rows, 128)
    at_side = pl.multiple_of((4 * core) * rows, 128)

    def remote(src, dst, send_sem, recv_sem, device):
        return pltpu.make_async_remote_copy(
            src_ref=src, dst_ref=dst, send_sem=send_sem, recv_sem=recv_sem,
            device_id=(device,), device_id_type=MESH,
        )

    def signal(sem, device):
        pl.semaphore_signal(sem, inc=1, device_id=(device,), device_id_type=MESH)

    barrier = pltpu.get_barrier_semaphore()
    signal(barrier, sib)

    @pl.when(jnp.logical_not(top))
    def _():
        signal(barrier, out)

    @pl.when(helper)
    def _():
        signal(barrier, helped_foot)
        signal(barrier, helped_top)

    locals_ = [
        pltpu.make_async_copy(src, dst, local_sem.at[i])
        for i, (src, dst) in enumerate(
            [
                (gvec_ref, gvec),
                (x_ref, both.at[pl.ds(0, rows)]),
                (table_ref, table),
                (val_ref, val),
                (cond_ref, cond),
            ]
        )
    ]
    for copy in locals_:
        copy.start()
    pl.semaphore_wait(barrier, jnp.where(top, 3, 2))

    blocks = [
        remote(x_ref.at[part], other.at[part], block_sem.at[0, i], block_sem.at[1, i], out)
        for i, part in enumerate(parts)
    ]
    passes = [
        remote(x_ref.at[part], relay.at[part], block_sem.at[0, i], relay_sem.at[1, i], my_helper)
        for i, part in enumerate(parts)
    ]

    @pl.when(top)
    def _():
        signal(helper_ready, top_helper)
        signal(foot_ready, out)

    beside = remote(x_ref, both.at[pl.ds(rows, rows)], sib_sem.at[0], sib_sem.at[1], sib)

    @pl.when(foot)
    def _():
        for copy in passes:
            copy.start()

    @pl.when(jnp.logical_not(foot))
    def _():
        for copy in blocks:
            copy.start()

    beside.start()

    onward = [
        remote(relay.at[part], other.at[part], relay_sem.at[0, i], block_sem.at[1, i], helped_top)
        for i, part in enumerate(parts)
    ]

    def hand_on(i):
        @pl.when(helper)
        def _():
            passes[i].wait_recv()
            onward[i].start()

    locals_[0].wait()
    total = jnp.zeros((1, width), jnp.float32)
    for axis, shift in enumerate((0.1, 0.2, 0.3)):
        component = gvec[axis : axis + 1, :].astype(jnp.float32) + jnp.float32(shift)
        total = total + component * component
    inverse = 1.0 / total
    weight[...] = jnp.sqrt(inverse / jnp.mean(inverse))

    def scale(ref, first, count):
        def body(step, carry):
            part = pl.ds(pl.multiple_of(first + step * SCALE_ROWS, SCALE_ROWS), SCALE_ROWS)
            ref[part, :] = (ref[part, :].astype(jnp.float32) * weight[...]).astype(jnp.bfloat16)
            return carry

        lax.fori_loop(0, count // SCALE_ROWS, body, 0)

    factor = 2.0 / jnp.sqrt(jnp.full((1, 1), width, jnp.float32))

    for copy in locals_[2:]:
        copy.wait()
    nk, nv = val.shape[1], val.shape[0]
    padded = jnp.concatenate([val[...], jnp.zeros((8 - nv, nk), jnp.float32)], axis=0)
    terms[...] = jnp.concatenate(in_three(cond[...]) + in_three(padded), axis=0).astype(jnp.bfloat16)
    k_row = table[2:3, :]

    def match(step, carry):
        first = pl.multiple_of(step * KSTEP, KSTEP)
        numbers = lax.broadcasted_iota(jnp.int32, (KSTEP, rows), 0) + first
        matches = (numbers == k_row).astype(jnp.float32).astype(jnp.bfloat16)
        return carry + jnp.dot(
            terms[:, pl.ds(first, KSTEP)], matches, preferred_element_type=jnp.float32
        )

    picked = lax.fori_loop(0, nk // KSTEP, match, jnp.zeros((48, rows), jnp.float32))
    of_cond = picked[0:8, :] + picked[8:16, :] + picked[16:24, :]
    of_val = picked[24:32, :] + picked[32:40, :] + picked[40:48, :]

    def band(values, chosen):
        bands = lax.broadcasted_iota(jnp.int32, values.shape, 0)
        return jnp.sum(jnp.where(bands == chosen, values, 0.0), axis=0, keepdims=True)

    energy[...] = band(of_cond, table[1:2, :]) - band(of_val, table[0:1, :])

    locals_[1].wait()
    scale(both, 0, rows)

    def own(step, carry):
        first = pl.multiple_of(step * CHUNK, CHUNK)
        part = pl.ds(first, CHUNK)
        tile = factor * times_transposed(both[part, :], both[pl.ds(0, rows), :])
        i = lax.broadcasted_iota(jnp.int32, tile.shape, 0) + first
        j = lax.broadcasted_iota(jnp.int32, tile.shape, 1)
        out_ref[part, pl.ds(at_own, rows)] = tile + jnp.where(i == j, energy[...], 0.0)
        return carry

    lax.fori_loop(0, chunks, own, 0)

    beside.wait_recv()
    scale(both, rows, rows)

    def near(step, carry):
        part = pl.ds(pl.multiple_of(step * CHUNK, CHUNK), CHUNK)
        out_ref[part, pl.ds(at_sib, rows)] = factor * times_transposed(
            both[part, :], both[pl.ds(rows, rows), :]
        )
        return carry

    lax.fori_loop(0, chunks, near, 0)

    @pl.when(helper)
    def _():
        pl.semaphore_wait(helper_ready, 1)

    @pl.when(foot)
    def _():
        pl.semaphore_wait(foot_ready, 1)

    hand_on(0)

    sides, backs, group_rows = [], [], []
    for i, part in enumerate(parts):
        blocks[i].wait_recv()
        scale(other, part.start, part.size)
        product = factor * times_transposed(other[part, :], both[pl.ds(rows, rows), :])
        far_out[part, :] = product.astype(jnp.bfloat16)
        group_rows.append(product)
        backs.append(
            remote(far_out.at[part], far_in.at[part], back_sem.at[0, i], back_sem.at[1, i], out)
        )
        pl.when(jnp.logical_not(foot))(backs[-1].start)
        if i + 1 < len(parts):
            hand_on(i + 1)
        end = part.start + part.size
        if end % CHUNK:
            continue
        group = end // CHUNK - 1
        chunk = pl.ds(end - CHUNK, CHUNK)
        far[group] = jnp.concatenate(group_rows, axis=0).T
        group_rows.clear()
        sides.append(
            remote(
                far.at[group],
                out_ref.at[:, pl.ds(pl.multiple_of(at_side + end - CHUNK, 128), CHUNK)],
                side_sem.at[0, group], side_sem.at[1, group], sib,
            )
        )
        sides[-1].start()
        out_ref[:, pl.ds(pl.multiple_of(at_out + end - CHUNK, 128), CHUNK)] = (
            factor * times_transposed(both[pl.ds(0, rows), :], other[chunk, :])
        )

    for i, part in enumerate(parts):
        backs[i].wait_recv()
        out_ref[part, pl.ds(at_far, rows)] = far_in[part, :].astype(jnp.float32)
        if i == FOOT_WAITS:

            @pl.when(foot)
            def _():
                for copy in backs:
                    copy.start()

    for copy in sides:
        copy.wait()
    for copy in blocks + backs + [beside]:
        copy.wait_send()

    @pl.when(helper)
    def _():
        for copy in onward:
            copy.wait_send()


def shards(pair_density, table, gvec, val_energy, cond_energy):
    rows, width = pair_density.shape
    n = lax.axis_size("blk")
    nk, nv = val_energy.shape
    nc = cond_energy.shape[1]
    chunks = rows // CHUNK
    anywhere = pl.BlockSpec(memory_space=pltpu.HBM)
    return pl.pallas_call(
        functools.partial(kernel, n),
        out_shape=jax.ShapeDtypeStruct((rows, 5 * rows), jnp.float32),
        in_specs=[anywhere] * 5,
        out_specs=pl.BlockSpec(memory_space=pltpu.VMEM),
        scratch_shapes=[
            pltpu.VMEM((2 * rows, width), jnp.bfloat16),
            pltpu.VMEM((rows, width), jnp.bfloat16),
            pltpu.VMEM((rows, width), jnp.bfloat16),
            pltpu.VMEM((chunks, rows, CHUNK), jnp.float32),
            pltpu.VMEM((rows, rows), jnp.bfloat16),
            pltpu.VMEM((rows, rows), jnp.bfloat16),
            pltpu.VMEM((3, rows), jnp.int32),
            pltpu.VMEM((3, width), jnp.int32),
            pltpu.VMEM((nv, nk), jnp.float32),
            pltpu.VMEM((nc, nk), jnp.float32),
            pltpu.VMEM((48, nk), jnp.bfloat16),
            pltpu.VMEM((1, width), jnp.float32),
            pltpu.VMEM((1, rows), jnp.float32),
            pltpu.SemaphoreType.DMA((5,)),
            pltpu.SemaphoreType.DMA((2,)),
            pltpu.SemaphoreType.DMA((2, len(PIECES))),
            pltpu.SemaphoreType.DMA((2, len(PIECES))),
            pltpu.SemaphoreType.DMA((2, chunks)),
            pltpu.SemaphoreType.DMA((2, len(PIECES))),
            pltpu.SemaphoreType.REGULAR,
            pltpu.SemaphoreType.REGULAR,
        ],
        compiler_params=pltpu.CompilerParams(
            collective_id=0, has_side_effects=True, vmem_limit_bytes=32 << 20
        ),
        name="band",
    )(*[pltpu.with_memory_space_constraint(v, pltpu.HBM) for v in (pair_density, table, gvec, val_energy.T, cond_energy.T)])


def solution(mesh):
    return jax.shard_map(
        shards,
        mesh=mesh,
        in_specs=(P("blk", None), P(None, "blk"), P(), P(), P()),
        out_specs=P("blk", None),
        check_vma=False,
    )
```

```python
import functools

import jax
import jax.numpy as jnp
from jax import lax
from jax.experimental import pallas as pl
from jax.experimental.pallas import tpu as pltpu
from jax.sharding import PartitionSpec as P

MESH = pl.DeviceIdType.MESH
CHUNK = 128
PIECES = (64, 64, 64, 64, 64, 32, 32)
FOOT_HOLDS = 4
LIFTED = 4
DIRECT = 5
COLUMN = 8
COLUMNS = 4
KSTEP = 512
SCALE_ROWS = 32


def times_transposed(left, right):
    return lax.dot_general(
        left, right, (((1,), (1,)), ((), ())), preferred_element_type=jnp.float32
    )


def in_three(values):
    high = values.astype(jnp.bfloat16).astype(jnp.float32)
    rest = values - high
    middle = rest.astype(jnp.bfloat16).astype(jnp.float32)
    return [high, middle, rest - middle]


def kernel(
    n, x_ref, table_ref, gvec_ref, val_ref, cond_ref, out_ref,
    both, other, relay, far, far_out, far_in, table, gvec, val, cond, terms, weight, energy,
    local_sem, sib_sem, block_sem, relay_sem, side_sem, back_sem, helper_ready, foot_ready, lift_ready,
):
    rows, width = x_ref.shape
    chunks = rows // CHUNK
    parts, first = [], 0
    for size in PIECES:
        parts.append(pl.ds(first, size))
        first += size
    me = lax.axis_index("blk")
    core = lax.rem(me, 2)
    level = lax.rem(me // 2, COLUMN)
    sib = me + 1 - 2 * core
    out = lax.rem(me + n - 1 + 2 * core, n)
    foot = jnp.logical_and(level == 0, core == 0)
    helper = jnp.logical_and(level == 0, core == 1)
    top = jnp.logical_and(level == COLUMN - 1, core == 1)
    my_helper = lax.rem(me + n - 2 * COLUMN + 1, n)
    helped_foot = lax.rem(me + 2 * COLUMN - 1, n)
    helped_top = lax.rem(me + 2 * COLUMN - 2, n)
    top_helper = lax.rem(me + n - 2 * COLUMN + 2, n)
    column = lax.rem(me // (2 * COLUMN), COLUMNS)
    first_foot = jnp.logical_and(foot, column == 0)
    last_helper = jnp.logical_and(helper, column == COLUMNS - 1)
    last_top = jnp.logical_and(top, column == COLUMNS - 1)
    lifter = jnp.logical_and(
        jnp.logical_and(level == COLUMN - 1, core == 0), column == 0
    )
    apart = 2 * COLUMN * (COLUMNS - 1) + 1
    my_lifter = lax.rem(me + n - apart, n)
    foot_lifter = lax.rem(me + n - apart - 1, n)
    lifted_top = lax.rem(me + apart, n)
    lifted_foot = lax.rem(me + apart + 1, n)
    at_own = 2 * rows
    at_sib = pl.multiple_of((3 - 2 * core) * rows, 128)
    at_out = pl.multiple_of((1 + 2 * core) * rows, 128)
    at_far = pl.multiple_of((4 * core) * rows, 128)
    at_side = pl.multiple_of((4 * core) * rows, 128)

    def remote(src, dst, send_sem, recv_sem, device):
        return pltpu.make_async_remote_copy(
            src_ref=src, dst_ref=dst, send_sem=send_sem, recv_sem=recv_sem,
            device_id=(device,), device_id_type=MESH,
        )

    def signal(sem, device):
        pl.semaphore_signal(sem, inc=1, device_id=(device,), device_id_type=MESH)

    barrier = pltpu.get_barrier_semaphore()
    signal(barrier, sib)

    @pl.when(jnp.logical_not(top))
    def _():
        signal(barrier, out)

    @pl.when(helper)
    def _():
        signal(barrier, helped_foot)
        signal(barrier, helped_top)

    @pl.when(last_top)
    def _():
        signal(barrier, my_lifter)

    @pl.when(first_foot)
    def _():
        signal(barrier, foot_lifter)

    locals_ = [
        pltpu.make_async_copy(src, dst, local_sem.at[i])
        for i, (src, dst) in enumerate(
            [
                (gvec_ref, gvec),
                (x_ref, both.at[pl.ds(0, rows)]),
                (table_ref, table),
                (val_ref, val),
                (cond_ref, cond),
            ]
        )
    ]
    for copy in locals_:
        copy.start()
    pl.semaphore_wait(barrier, jnp.where(lifter, 4, jnp.where(top, 3, 2)))

    blocks = [
        remote(x_ref.at[part], other.at[part], block_sem.at[0, i], block_sem.at[1, i], out)
        for i, part in enumerate(parts)
    ]
    passes = [
        remote(x_ref.at[part], relay.at[part], block_sem.at[0, i], relay_sem.at[1, i], my_helper)
        for i, part in enumerate(parts)
    ]

    @pl.when(top)
    def _():
        signal(helper_ready, top_helper)
        signal(foot_ready, out)

    beside = remote(x_ref, both.at[pl.ds(rows, rows)], sib_sem.at[0], sib_sem.at[1], sib)

    lift = remote(
        x_ref.at[parts[LIFTED]], relay.at[parts[LIFTED]],
        block_sem.at[0, LIFTED], relay_sem.at[1, LIFTED], my_lifter,
    )
    lift_on = remote(
        relay.at[parts[LIFTED]], other.at[parts[LIFTED]],
        relay_sem.at[0, LIFTED], block_sem.at[1, LIFTED], lifted_foot,
    )

    @pl.when(lifter)
    def _():
        signal(lift_ready, lifted_top)

    @pl.when(foot)
    def _():
        for i, copy in enumerate(passes):
            if i == DIRECT:
                pl.when(jnp.logical_not(first_foot))(copy.start)
            else:
                copy.start()

    @pl.when(jnp.logical_not(foot))
    def _():
        for i, copy in enumerate(blocks):
            if i == LIFTED:
                pl.when(jnp.logical_not(last_top))(copy.start)
            else:
                copy.start()

    beside.start()

    @pl.when(last_top)
    def _():
        pl.semaphore_wait(lift_ready, 1)
        lift.start()

    onward = [
        remote(relay.at[part], other.at[part], relay_sem.at[0, i], block_sem.at[1, i], helped_top)
        for i, part in enumerate(parts)
    ]

    def hands_on(i):
        if i == DIRECT:
            return jnp.logical_and(helper, jnp.logical_not(last_helper))
        return helper

    def hand_on(i):
        @pl.when(hands_on(i))
        def _():
            passes[i].wait_recv()
            onward[i].start()

    locals_[0].wait()
    total = jnp.zeros((1, width), jnp.float32)
    for axis, shift in enumerate((0.1, 0.2, 0.3)):
        component = gvec[axis : axis + 1, :].astype(jnp.float32) + jnp.float32(shift)
        total = total + component * component
    inverse = 1.0 / total
    weight[...] = jnp.sqrt(inverse / jnp.mean(inverse))

    def scale(ref, first, count):
        def body(step, carry):
            part = pl.ds(pl.multiple_of(first + step * SCALE_ROWS, SCALE_ROWS), SCALE_ROWS)
            ref[part, :] = (ref[part, :].astype(jnp.float32) * weight[...]).astype(jnp.bfloat16)
            return carry

        lax.fori_loop(0, count // SCALE_ROWS, body, 0)

    factor = 2.0 / jnp.sqrt(jnp.full((1, 1), width, jnp.float32))

    for copy in locals_[2:]:
        copy.wait()
    nk, nv = val.shape[1], val.shape[0]
    padded = jnp.concatenate([val[...], jnp.zeros((8 - nv, nk), jnp.float32)], axis=0)
    terms[...] = jnp.concatenate(in_three(cond[...]) + in_three(padded), axis=0).astype(jnp.bfloat16)
    k_row = table[2:3, :]

    def match(step, carry):
        first = pl.multiple_of(step * KSTEP, KSTEP)
        numbers = lax.broadcasted_iota(jnp.int32, (KSTEP, rows), 0) + first
        matches = (numbers == k_row).astype(jnp.float32).astype(jnp.bfloat16)
        return carry + jnp.dot(
            terms[:, pl.ds(first, KSTEP)], matches, preferred_element_type=jnp.float32
        )

    picked = lax.fori_loop(0, nk // KSTEP, match, jnp.zeros((48, rows), jnp.float32))
    of_cond = picked[0:8, :] + picked[8:16, :] + picked[16:24, :]
    of_val = picked[24:32, :] + picked[32:40, :] + picked[40:48, :]

    def band(values, chosen):
        bands = lax.broadcasted_iota(jnp.int32, values.shape, 0)
        return jnp.sum(jnp.where(bands == chosen, values, 0.0), axis=0, keepdims=True)

    energy[...] = band(of_cond, table[1:2, :]) - band(of_val, table[0:1, :])

    locals_[1].wait()
    scale(both, 0, rows)

    def own(step, carry):
        first = pl.multiple_of(step * CHUNK, CHUNK)
        part = pl.ds(first, CHUNK)
        tile = factor * times_transposed(both[part, :], both[pl.ds(0, rows), :])
        i = lax.broadcasted_iota(jnp.int32, tile.shape, 0) + first
        j = lax.broadcasted_iota(jnp.int32, tile.shape, 1)
        out_ref[part, pl.ds(at_own, rows)] = tile + jnp.where(i == j, energy[...], 0.0)
        return carry

    lax.fori_loop(0, chunks, own, 0)

    @pl.when(helper)
    def _():
        pl.semaphore_wait(helper_ready, 1)

    hand_on(0)

    beside.wait_recv()
    scale(both, rows, rows)

    def near(step, carry):
        part = pl.ds(pl.multiple_of(step * CHUNK, CHUNK), CHUNK)
        out_ref[part, pl.ds(at_sib, rows)] = factor * times_transposed(
            both[part, :], both[pl.ds(rows, rows), :]
        )
        return carry

    lax.fori_loop(0, chunks, near, 0)

    @pl.when(foot)
    def _():
        pl.semaphore_wait(foot_ready, 1)
        pl.when(first_foot)(blocks[DIRECT].start)

    sides, backs, group_rows = [], [], []
    for i, part in enumerate(parts):
        blocks[i].wait_recv()
        scale(other, part.start, part.size)
        product = factor * times_transposed(other[part, :], both[pl.ds(rows, rows), :])
        far_out[part, :] = product.astype(jnp.bfloat16)
        group_rows.append(product)
        backs.append(
            remote(far_out.at[part], far_in.at[part], back_sem.at[0, i], back_sem.at[1, i], out)
        )
        if i < FOOT_HOLDS:
            pl.when(jnp.logical_not(foot))(backs[i].start)
        else:
            if i == FOOT_HOLDS:

                @pl.when(foot)
                def _():
                    for copy in backs[:FOOT_HOLDS]:
                        copy.start()

            backs[i].start()
        if i + 1 < len(parts):
            hand_on(i + 1)
        if i == 1:

            @pl.when(lifter)
            def _():
                lift.wait_recv()
                lift_on.start()

        end = part.start + part.size
        if end % CHUNK:
            continue
        group = end // CHUNK - 1
        chunk = pl.ds(end - CHUNK, CHUNK)
        far[group] = jnp.concatenate(group_rows, axis=0).T
        group_rows.clear()
        sides.append(
            remote(
                far.at[group],
                out_ref.at[:, pl.ds(pl.multiple_of(at_side + end - CHUNK, 128), CHUNK)],
                side_sem.at[0, group], side_sem.at[1, group], sib,
            )
        )
        sides[-1].start()
        out_ref[:, pl.ds(pl.multiple_of(at_out + end - CHUNK, 128), CHUNK)] = (
            factor * times_transposed(both[pl.ds(0, rows), :], other[chunk, :])
        )

    for i, part in enumerate(parts):
        backs[i].wait_recv()
        out_ref[part, pl.ds(at_far, rows)] = far_in[part, :].astype(jnp.float32)
    for copy in sides:
        copy.wait()
    for copy in blocks + backs + [beside]:
        copy.wait_send()

    for i, copy in enumerate(onward):
        pl.when(hands_on(i))(copy.wait_send)
    pl.when(lifter)(lift_on.wait_send)


def shards(pair_density, table, gvec, val_energy, cond_energy):
    rows, width = pair_density.shape
    n = lax.axis_size("blk")
    nk, nv = val_energy.shape
    nc = cond_energy.shape[1]
    chunks = rows // CHUNK
    anywhere = pl.BlockSpec(memory_space=pltpu.HBM)
    return pl.pallas_call(
        functools.partial(kernel, n),
        out_shape=jax.ShapeDtypeStruct((rows, 5 * rows), jnp.float32),
        in_specs=[anywhere] * 5,
        out_specs=pl.BlockSpec(memory_space=pltpu.VMEM),
        scratch_shapes=[
            pltpu.VMEM((2 * rows, width), jnp.bfloat16),
            pltpu.VMEM((rows, width), jnp.bfloat16),
            pltpu.VMEM((rows, width), jnp.bfloat16),
            pltpu.VMEM((chunks, rows, CHUNK), jnp.float32),
            pltpu.VMEM((rows, rows), jnp.bfloat16),
            pltpu.VMEM((rows, rows), jnp.bfloat16),
            pltpu.VMEM((3, rows), jnp.int32),
            pltpu.VMEM((3, width), jnp.int32),
            pltpu.VMEM((nv, nk), jnp.float32),
            pltpu.VMEM((nc, nk), jnp.float32),
            pltpu.VMEM((48, nk), jnp.bfloat16),
            pltpu.VMEM((1, width), jnp.float32),
            pltpu.VMEM((1, rows), jnp.float32),
            pltpu.SemaphoreType.DMA((5,)),
            pltpu.SemaphoreType.DMA((2,)),
            pltpu.SemaphoreType.DMA((2, len(PIECES))),
            pltpu.SemaphoreType.DMA((2, len(PIECES))),
            pltpu.SemaphoreType.DMA((2, chunks)),
            pltpu.SemaphoreType.DMA((2, len(PIECES))),
            pltpu.SemaphoreType.REGULAR,
            pltpu.SemaphoreType.REGULAR,
            pltpu.SemaphoreType.REGULAR,
        ],
        compiler_params=pltpu.CompilerParams(
            collective_id=0, has_side_effects=True, vmem_limit_bytes=32 << 20
        ),
        name="band",
    )(*[pltpu.with_memory_space_constraint(v, pltpu.HBM) for v in (pair_density, table, gvec, val_energy.T, cond_energy.T)])


def solution(mesh):
    return jax.shard_map(
        shards,
        mesh=mesh,
        in_specs=(P("blk", None), P(None, "blk"), P(), P(), P()),
        out_specs=P("blk", None),
        check_vma=False,
    )
```

```python
import functools

import jax
import jax.numpy as jnp
from jax import lax
from jax.experimental import pallas as pl
from jax.experimental.pallas import tpu as pltpu
from jax.sharding import PartitionSpec as P

MESH = pl.DeviceIdType.MESH
CHUNK = 128
PIECES = (64, 64, 64, 64, 64, 32, 32)
FOOT_HOLDS = 5
LIFTED = 4
DIRECT = 5
COLUMN = 8
COLUMNS = 4
KSTEP = 512
SCALE_ROWS = 32


def times_transposed(left, right):
    return lax.dot_general(
        left, right, (((1,), (1,)), ((), ())), preferred_element_type=jnp.float32
    )


def in_three(values):
    high = values.astype(jnp.bfloat16).astype(jnp.float32)
    rest = values - high
    middle = rest.astype(jnp.bfloat16).astype(jnp.float32)
    return [high, middle, rest - middle]


def kernel(
    n, x_ref, table_ref, gvec_ref, val_ref, cond_ref, out_ref,
    both, other, relay, far, far_out, far_in, table, gvec, val, cond, terms, weight, energy,
    local_sem, sib_sem, block_sem, relay_sem, side_sem, back_sem, helper_ready, foot_ready, lift_ready,
):
    rows, width = x_ref.shape
    chunks = rows // CHUNK
    parts, first = [], 0
    for size in PIECES:
        parts.append(pl.ds(first, size))
        first += size
    me = lax.axis_index("blk")
    core = lax.rem(me, 2)
    level = lax.rem(me // 2, COLUMN)
    sib = me + 1 - 2 * core
    out = lax.rem(me + n - 1 + 2 * core, n)
    foot = jnp.logical_and(level == 0, core == 0)
    helper = jnp.logical_and(level == 0, core == 1)
    top = jnp.logical_and(level == COLUMN - 1, core == 1)
    my_helper = lax.rem(me + n - 2 * COLUMN + 1, n)
    helped_foot = lax.rem(me + 2 * COLUMN - 1, n)
    helped_top = lax.rem(me + 2 * COLUMN - 2, n)
    top_helper = lax.rem(me + n - 2 * COLUMN + 2, n)
    column = lax.rem(me // (2 * COLUMN), COLUMNS)
    first_foot = jnp.logical_and(foot, column == 0)
    last_helper = jnp.logical_and(helper, column == COLUMNS - 1)
    last_top = jnp.logical_and(top, column == COLUMNS - 1)
    lifter = jnp.logical_and(
        jnp.logical_and(level == COLUMN - 1, core == 0), column == 0
    )
    apart = 2 * COLUMN * (COLUMNS - 1) + 1
    my_lifter = lax.rem(me + n - apart, n)
    foot_lifter = lax.rem(me + n - apart - 1, n)
    lifted_top = lax.rem(me + apart, n)
    lifted_foot = lax.rem(me + apart + 1, n)
    at_own = 2 * rows
    at_sib = pl.multiple_of((3 - 2 * core) * rows, 128)
    at_out = pl.multiple_of((1 + 2 * core) * rows, 128)
    at_far = pl.multiple_of((4 * core) * rows, 128)
    at_side = pl.multiple_of((4 * core) * rows, 128)

    def remote(src, dst, send_sem, recv_sem, device):
        return pltpu.make_async_remote_copy(
            src_ref=src, dst_ref=dst, send_sem=send_sem, recv_sem=recv_sem,
            device_id=(device,), device_id_type=MESH,
        )

    def signal(sem, device):
        pl.semaphore_signal(sem, inc=1, device_id=(device,), device_id_type=MESH)

    barrier = pltpu.get_barrier_semaphore()
    signal(barrier, sib)

    @pl.when(jnp.logical_not(top))
    def _():
        signal(barrier, out)

    @pl.when(helper)
    def _():
        signal(barrier, helped_foot)
        signal(barrier, helped_top)

    @pl.when(last_top)
    def _():
        signal(barrier, my_lifter)

    @pl.when(first_foot)
    def _():
        signal(barrier, foot_lifter)

    locals_ = [
        pltpu.make_async_copy(src, dst, local_sem.at[i])
        for i, (src, dst) in enumerate(
            [
                (gvec_ref, gvec),
                (x_ref, both.at[pl.ds(0, rows)]),
                (table_ref, table),
                (val_ref, val),
                (cond_ref, cond),
            ]
        )
    ]
    for copy in locals_:
        copy.start()
    pl.semaphore_wait(barrier, jnp.where(lifter, 4, jnp.where(top, 3, 2)))

    blocks = [
        remote(x_ref.at[part], other.at[part], block_sem.at[0, i], block_sem.at[1, i], out)
        for i, part in enumerate(parts)
    ]
    passes = [
        remote(x_ref.at[part], relay.at[part], block_sem.at[0, i], relay_sem.at[1, i], my_helper)
        for i, part in enumerate(parts)
    ]

    @pl.when(top)
    def _():
        signal(helper_ready, top_helper)
        signal(foot_ready, out)

    beside = remote(x_ref, both.at[pl.ds(rows, rows)], sib_sem.at[0], sib_sem.at[1], sib)

    lift = remote(
        x_ref.at[parts[LIFTED]], relay.at[parts[LIFTED]],
        block_sem.at[0, LIFTED], relay_sem.at[1, LIFTED], my_lifter,
    )
    lift_on = remote(
        relay.at[parts[LIFTED]], other.at[parts[LIFTED]],
        relay_sem.at[0, LIFTED], block_sem.at[1, LIFTED], lifted_foot,
    )

    @pl.when(lifter)
    def _():
        signal(lift_ready, lifted_top)

    @pl.when(foot)
    def _():
        for i, copy in enumerate(passes):
            if i == DIRECT:
                pl.when(jnp.logical_not(first_foot))(copy.start)
            else:
                copy.start()

    @pl.when(jnp.logical_not(foot))
    def _():
        for i, copy in enumerate(blocks):
            if i == LIFTED:
                pl.when(jnp.logical_not(last_top))(copy.start)
            else:
                copy.start()

    beside.start()

    @pl.when(last_top)
    def _():
        pl.semaphore_wait(lift_ready, 1)
        lift.start()

    onward = [
        remote(relay.at[part], other.at[part], relay_sem.at[0, i], block_sem.at[1, i], helped_top)
        for i, part in enumerate(parts)
    ]

    def hands_on(i):
        if i == DIRECT:
            return jnp.logical_and(helper, jnp.logical_not(last_helper))
        return helper

    def hand_on(i):
        @pl.when(hands_on(i))
        def _():
            passes[i].wait_recv()
            onward[i].start()

    locals_[0].wait()
    total = jnp.zeros((1, width), jnp.float32)
    for axis, shift in enumerate((0.1, 0.2, 0.3)):
        component = gvec[axis : axis + 1, :].astype(jnp.float32) + jnp.float32(shift)
        total = total + component * component
    inverse = 1.0 / total
    weight[...] = jnp.sqrt(inverse / jnp.mean(inverse))

    def scale(ref, first, count):
        def body(step, carry):
            part = pl.ds(pl.multiple_of(first + step * SCALE_ROWS, SCALE_ROWS), SCALE_ROWS)
            ref[part, :] = (ref[part, :].astype(jnp.float32) * weight[...]).astype(jnp.bfloat16)
            return carry

        lax.fori_loop(0, count // SCALE_ROWS, body, 0)

    factor = 2.0 / jnp.sqrt(jnp.full((1, 1), width, jnp.float32))

    for copy in locals_[2:]:
        copy.wait()
    nk, nv = val.shape[1], val.shape[0]
    padded = jnp.concatenate([val[...], jnp.zeros((8 - nv, nk), jnp.float32)], axis=0)
    terms[...] = jnp.concatenate(in_three(cond[...]) + in_three(padded), axis=0).astype(jnp.bfloat16)
    k_row = table[2:3, :]

    def match(step, carry):
        first = pl.multiple_of(step * KSTEP, KSTEP)
        numbers = lax.broadcasted_iota(jnp.int32, (KSTEP, rows), 0) + first
        matches = (numbers == k_row).astype(jnp.float32).astype(jnp.bfloat16)
        return carry + jnp.dot(
            terms[:, pl.ds(first, KSTEP)], matches, preferred_element_type=jnp.float32
        )

    picked = lax.fori_loop(0, nk // KSTEP, match, jnp.zeros((48, rows), jnp.float32))
    of_cond = picked[0:8, :] + picked[8:16, :] + picked[16:24, :]
    of_val = picked[24:32, :] + picked[32:40, :] + picked[40:48, :]

    def band(values, chosen):
        bands = lax.broadcasted_iota(jnp.int32, values.shape, 0)
        return jnp.sum(jnp.where(bands == chosen, values, 0.0), axis=0, keepdims=True)

    energy[...] = band(of_cond, table[1:2, :]) - band(of_val, table[0:1, :])

    locals_[1].wait()
    scale(both, 0, rows)

    def own(step, carry):
        first = pl.multiple_of(step * CHUNK, CHUNK)
        part = pl.ds(first, CHUNK)
        tile = factor * times_transposed(both[part, :], both[pl.ds(0, rows), :])
        i = lax.broadcasted_iota(jnp.int32, tile.shape, 0) + first
        j = lax.broadcasted_iota(jnp.int32, tile.shape, 1)
        out_ref[part, pl.ds(at_own, rows)] = tile + jnp.where(i == j, energy[...], 0.0)
        return carry

    lax.fori_loop(0, chunks, own, 0)

    @pl.when(helper)
    def _():
        pl.semaphore_wait(helper_ready, 1)

    hand_on(0)

    beside.wait_recv()
    scale(both, rows, rows)

    def near(step, carry):
        part = pl.ds(pl.multiple_of(step * CHUNK, CHUNK), CHUNK)
        out_ref[part, pl.ds(at_sib, rows)] = factor * times_transposed(
            both[part, :], both[pl.ds(rows, rows), :]
        )
        return carry

    lax.fori_loop(0, chunks, near, 0)

    @pl.when(foot)
    def _():
        pl.semaphore_wait(foot_ready, 1)
        pl.when(first_foot)(blocks[DIRECT].start)

    sides, backs, group_rows = [], [], []
    for i, part in enumerate(parts):
        blocks[i].wait_recv()
        scale(other, part.start, part.size)
        product = factor * times_transposed(other[part, :], both[pl.ds(rows, rows), :])
        far_out[part, :] = product.astype(jnp.bfloat16)
        group_rows.append(product)
        backs.append(
            remote(far_out.at[part], far_in.at[part], back_sem.at[0, i], back_sem.at[1, i], out)
        )
        if i < FOOT_HOLDS:
            pl.when(jnp.logical_not(foot))(backs[i].start)
        else:
            if i == FOOT_HOLDS:

                @pl.when(foot)
                def _():
                    for copy in backs[:FOOT_HOLDS]:
                        copy.start()

            backs[i].start()
        if i + 1 < len(parts):
            hand_on(i + 1)
        if i == 0:

            @pl.when(lifter)
            def _():
                lift.wait_recv()
                lift_on.start()

        end = part.start + part.size
        if end % CHUNK:
            continue
        group = end // CHUNK - 1
        chunk = pl.ds(end - CHUNK, CHUNK)
        far[group] = jnp.concatenate(group_rows, axis=0).T
        group_rows.clear()
        sides.append(
            remote(
                far.at[group],
                out_ref.at[:, pl.ds(pl.multiple_of(at_side + end - CHUNK, 128), CHUNK)],
                side_sem.at[0, group], side_sem.at[1, group], sib,
            )
        )
        sides[-1].start()
        out_ref[:, pl.ds(pl.multiple_of(at_out + end - CHUNK, 128), CHUNK)] = (
            factor * times_transposed(both[pl.ds(0, rows), :], other[chunk, :])
        )

    def came_back(i):
        backs[i].wait_recv()
        out_ref[parts[i], pl.ds(at_far, rows)] = far_in[parts[i], :].astype(jnp.float32)

    last = len(parts) - 1
    for copy in blocks + [beside]:
        copy.wait_send()
    for i, copy in enumerate(onward):
        pl.when(hands_on(i))(copy.wait_send)
    pl.when(lifter)(lift_on.wait_send)
    for i in range(last):
        came_back(i)
    for copy in backs[: last - 1]:
        copy.wait_send()
    for copy in sides:
        copy.wait()
    came_back(last)
    for copy in backs[last - 1 :]:
        copy.wait_send()


def shards(pair_density, table, gvec, val_energy, cond_energy):
    rows, width = pair_density.shape
    n = lax.axis_size("blk")
    nk, nv = val_energy.shape
    nc = cond_energy.shape[1]
    chunks = rows // CHUNK
    anywhere = pl.BlockSpec(memory_space=pltpu.HBM)
    return pl.pallas_call(
        functools.partial(kernel, n),
        out_shape=jax.ShapeDtypeStruct((rows, 5 * rows), jnp.float32),
        in_specs=[anywhere] * 5,
        out_specs=pl.BlockSpec(memory_space=pltpu.VMEM),
        scratch_shapes=[
            pltpu.VMEM((2 * rows, width), jnp.bfloat16),
            pltpu.VMEM((rows, width), jnp.bfloat16),
            pltpu.VMEM((rows, width), jnp.bfloat16),
            pltpu.VMEM((chunks, rows, CHUNK), jnp.float32),
            pltpu.VMEM((rows, rows), jnp.bfloat16),
            pltpu.VMEM((rows, rows), jnp.bfloat16),
            pltpu.VMEM((3, rows), jnp.int32),
            pltpu.VMEM((3, width), jnp.int32),
            pltpu.VMEM((nv, nk), jnp.float32),
            pltpu.VMEM((nc, nk), jnp.float32),
            pltpu.VMEM((48, nk), jnp.bfloat16),
            pltpu.VMEM((1, width), jnp.float32),
            pltpu.VMEM((1, rows), jnp.float32),
            pltpu.SemaphoreType.DMA((5,)),
            pltpu.SemaphoreType.DMA((2,)),
            pltpu.SemaphoreType.DMA((2, len(PIECES))),
            pltpu.SemaphoreType.DMA((2, len(PIECES))),
            pltpu.SemaphoreType.DMA((2, chunks)),
            pltpu.SemaphoreType.DMA((2, len(PIECES))),
            pltpu.SemaphoreType.REGULAR,
            pltpu.SemaphoreType.REGULAR,
            pltpu.SemaphoreType.REGULAR,
        ],
        compiler_params=pltpu.CompilerParams(
            collective_id=0, has_side_effects=True, vmem_limit_bytes=32 << 20
        ),
        name="band",
    )(*[pltpu.with_memory_space_constraint(v, pltpu.HBM) for v in (pair_density, table, gvec, val_energy.T, cond_energy.T)])


def solution(mesh):
    return jax.shard_map(
        shards,
        mesh=mesh,
        in_specs=(P("blk", None), P(None, "blk"), P(), P(), P()),
        out_specs=P("blk", None),
        check_vma=False,
    )
```

```python
import functools

import jax
import jax.numpy as jnp
from jax import lax
from jax.experimental import pallas as pl
from jax.experimental.pallas import tpu as pltpu
from jax.sharding import PartitionSpec as P

MESH = pl.DeviceIdType.MESH
CHUNK = 128
PIECES = (64, 64, 64, 64, 64, 32, 32)
FOOT_HOLDS = 5
LIFTED = 4
DIRECT = 5
COLUMN = 8
COLUMNS = 4
LIFTER = 1
KSTEP = 512
SCALE_ROWS = 32


def times_transposed(left, right):
    return lax.dot_general(
        left, right, (((1,), (1,)), ((), ())), preferred_element_type=jnp.float32
    )


def in_three(values):
    high = values.astype(jnp.bfloat16).astype(jnp.float32)
    rest = values - high
    middle = rest.astype(jnp.bfloat16).astype(jnp.float32)
    return [high, middle, rest - middle]


def kernel(
    n, x_ref, table_ref, gvec_ref, val_ref, cond_ref, out_ref,
    both, other, relay, far, far_out, far_in, table, gvec, val, cond, terms, weight, energy,
    local_sem, sib_sem, block_sem, relay_sem, side_sem, back_sem, helper_ready, foot_ready, lift_ready,
):
    rows, width = x_ref.shape
    chunks = rows // CHUNK
    parts, first = [], 0
    for size in PIECES:
        parts.append(pl.ds(first, size))
        first += size
    me = lax.axis_index("blk")
    core = lax.rem(me, 2)
    level = lax.rem(me // 2, COLUMN)
    sib = me + 1 - 2 * core
    out = lax.rem(me + n - 1 + 2 * core, n)
    foot = jnp.logical_and(level == 0, core == 0)
    helper = jnp.logical_and(level == 0, core == 1)
    top = jnp.logical_and(level == COLUMN - 1, core == 1)
    my_helper = lax.rem(me + n - 2 * COLUMN + 1, n)
    helped_foot = lax.rem(me + 2 * COLUMN - 1, n)
    helped_top = lax.rem(me + 2 * COLUMN - 2, n)
    top_helper = lax.rem(me + n - 2 * COLUMN + 2, n)
    column = lax.rem(me // (2 * COLUMN), COLUMNS)
    first_foot = jnp.logical_and(foot, column == 0)
    last_helper = jnp.logical_and(helper, column == COLUMNS - 1)
    last_top = jnp.logical_and(top, column == COLUMNS - 1)
    lifter = jnp.logical_and(
        jnp.logical_and(level == COLUMN - 1, core == 0), column == LIFTER
    )
    apart = 2 * COLUMN * (COLUMNS - 1 - LIFTER) + 1
    my_lifter = lax.rem(me + n - apart, n)
    foot_lifter = lax.rem(me + n - apart - 1, n)
    lifted_top = lax.rem(me + apart, n)
    lifted_foot = lax.rem(me + apart + 1, n)
    at_own = 2 * rows
    at_sib = pl.multiple_of((3 - 2 * core) * rows, 128)
    at_out = pl.multiple_of((1 + 2 * core) * rows, 128)
    at_far = pl.multiple_of((4 * core) * rows, 128)
    at_side = pl.multiple_of((4 * core) * rows, 128)

    def remote(src, dst, send_sem, recv_sem, device):
        return pltpu.make_async_remote_copy(
            src_ref=src, dst_ref=dst, send_sem=send_sem, recv_sem=recv_sem,
            device_id=(device,), device_id_type=MESH,
        )

    def signal(sem, device):
        pl.semaphore_signal(sem, inc=1, device_id=(device,), device_id_type=MESH)

    barrier = pltpu.get_barrier_semaphore()
    signal(barrier, sib)

    @pl.when(jnp.logical_not(top))
    def _():
        signal(barrier, out)

    @pl.when(helper)
    def _():
        signal(barrier, helped_foot)
        signal(barrier, helped_top)

    @pl.when(last_top)
    def _():
        signal(barrier, my_lifter)

    @pl.when(first_foot)
    def _():
        signal(barrier, foot_lifter)

    locals_ = [
        pltpu.make_async_copy(src, dst, local_sem.at[i])
        for i, (src, dst) in enumerate(
            [
                (gvec_ref, gvec),
                (x_ref, both.at[pl.ds(0, rows)]),
                (table_ref, table),
                (val_ref, val),
                (cond_ref, cond),
            ]
        )
    ]
    for copy in locals_:
        copy.start()
    pl.semaphore_wait(barrier, jnp.where(lifter, 4, jnp.where(top, 3, 2)))

    blocks = [
        remote(x_ref.at[part], other.at[part], block_sem.at[0, i], block_sem.at[1, i], out)
        for i, part in enumerate(parts)
    ]
    passes = [
        remote(x_ref.at[part], relay.at[part], block_sem.at[0, i], relay_sem.at[1, i], my_helper)
        for i, part in enumerate(parts)
    ]

    @pl.when(top)
    def _():
        signal(helper_ready, top_helper)
        signal(foot_ready, out)

    beside = remote(x_ref, both.at[pl.ds(rows, rows)], sib_sem.at[0], sib_sem.at[1], sib)

    lift = remote(
        x_ref.at[parts[LIFTED]], relay.at[parts[LIFTED]],
        block_sem.at[0, LIFTED], relay_sem.at[1, LIFTED], my_lifter,
    )
    lift_on = remote(
        relay.at[parts[LIFTED]], other.at[parts[LIFTED]],
        relay_sem.at[0, LIFTED], block_sem.at[1, LIFTED], lifted_foot,
    )

    @pl.when(lifter)
    def _():
        signal(lift_ready, lifted_top)

    @pl.when(foot)
    def _():
        for i, copy in enumerate(passes):
            if i == DIRECT:
                pl.when(jnp.logical_not(first_foot))(copy.start)
            else:
                copy.start()

    @pl.when(jnp.logical_not(foot))
    def _():
        for i, copy in enumerate(blocks):
            if i == LIFTED:
                pl.when(jnp.logical_not(last_top))(copy.start)
            else:
                copy.start()

    beside.start()

    @pl.when(last_top)
    def _():
        pl.semaphore_wait(lift_ready, 1)
        lift.start()

    onward = [
        remote(relay.at[part], other.at[part], relay_sem.at[0, i], block_sem.at[1, i], helped_top)
        for i, part in enumerate(parts)
    ]

    def hands_on(i):
        if i == DIRECT:
            return jnp.logical_and(helper, jnp.logical_not(last_helper))
        return helper

    def hand_on(i):
        @pl.when(hands_on(i))
        def _():
            passes[i].wait_recv()
            onward[i].start()

    locals_[0].wait()
    total = jnp.zeros((1, width), jnp.float32)
    for axis, shift in enumerate((0.1, 0.2, 0.3)):
        component = gvec[axis : axis + 1, :].astype(jnp.float32) + jnp.float32(shift)
        total = total + component * component
    inverse = 1.0 / total
    weight[...] = jnp.sqrt(inverse / jnp.mean(inverse))

    def scale(ref, first, count):
        def body(step, carry):
            part = pl.ds(pl.multiple_of(first + step * SCALE_ROWS, SCALE_ROWS), SCALE_ROWS)
            ref[part, :] = (ref[part, :].astype(jnp.float32) * weight[...]).astype(jnp.bfloat16)
            return carry

        lax.fori_loop(0, count // SCALE_ROWS, body, 0)

    factor = 2.0 / jnp.sqrt(jnp.full((1, 1), width, jnp.float32))

    for copy in locals_[2:]:
        copy.wait()
    nk, nv = val.shape[1], val.shape[0]
    padded = jnp.concatenate([val[...], jnp.zeros((8 - nv, nk), jnp.float32)], axis=0)
    terms[...] = jnp.concatenate(in_three(cond[...]) + in_three(padded), axis=0).astype(jnp.bfloat16)
    k_row = table[2:3, :]

    def match(step, carry):
        first = pl.multiple_of(step * KSTEP, KSTEP)
        numbers = lax.broadcasted_iota(jnp.int32, (KSTEP, rows), 0) + first
        matches = (numbers == k_row).astype(jnp.float32).astype(jnp.bfloat16)
        return carry + jnp.dot(
            terms[:, pl.ds(first, KSTEP)], matches, preferred_element_type=jnp.float32
        )

    picked = lax.fori_loop(0, nk // KSTEP, match, jnp.zeros((48, rows), jnp.float32))
    of_cond = picked[0:8, :] + picked[8:16, :] + picked[16:24, :]
    of_val = picked[24:32, :] + picked[32:40, :] + picked[40:48, :]

    def band(values, chosen):
        bands = lax.broadcasted_iota(jnp.int32, values.shape, 0)
        return jnp.sum(jnp.where(bands == chosen, values, 0.0), axis=0, keepdims=True)

    energy[...] = band(of_cond, table[1:2, :]) - band(of_val, table[0:1, :])

    locals_[1].wait()
    scale(both, 0, rows)

    def own(step, carry):
        first = pl.multiple_of(step * CHUNK, CHUNK)
        part = pl.ds(first, CHUNK)
        tile = factor * times_transposed(both[part, :], both[pl.ds(0, rows), :])
        i = lax.broadcasted_iota(jnp.int32, tile.shape, 0) + first
        j = lax.broadcasted_iota(jnp.int32, tile.shape, 1)
        out_ref[part, pl.ds(at_own, rows)] = tile + jnp.where(i == j, energy[...], 0.0)
        return carry

    lax.fori_loop(0, chunks, own, 0)

    @pl.when(helper)
    def _():
        pl.semaphore_wait(helper_ready, 1)

    hand_on(0)

    beside.wait_recv()
    scale(both, rows, rows)

    def near(step, carry):
        part = pl.ds(pl.multiple_of(step * CHUNK, CHUNK), CHUNK)
        out_ref[part, pl.ds(at_sib, rows)] = factor * times_transposed(
            both[part, :], both[pl.ds(rows, rows), :]
        )
        return carry

    lax.fori_loop(0, chunks, near, 0)

    @pl.when(foot)
    def _():
        pl.semaphore_wait(foot_ready, 1)
        pl.when(first_foot)(blocks[DIRECT].start)

    sides, backs, group_rows = [], [], []
    for i, part in enumerate(parts):
        blocks[i].wait_recv()
        scale(other, part.start, part.size)
        product = factor * times_transposed(other[part, :], both[pl.ds(rows, rows), :])
        far_out[part, :] = product.astype(jnp.bfloat16)
        group_rows.append(product)
        backs.append(
            remote(far_out.at[part], far_in.at[part], back_sem.at[0, i], back_sem.at[1, i], out)
        )
        if i < FOOT_HOLDS:
            pl.when(jnp.logical_not(foot))(backs[i].start)
        else:
            if i == FOOT_HOLDS:

                @pl.when(foot)
                def _():
                    for copy in backs[:FOOT_HOLDS]:
                        copy.start()

            backs[i].start()
        if i + 1 < len(parts):
            hand_on(i + 1)
        if i == 0:

            @pl.when(lifter)
            def _():
                lift.wait_recv()
                lift_on.start()

        end = part.start + part.size
        if end % CHUNK:
            continue
        group = end // CHUNK - 1
        chunk = pl.ds(end - CHUNK, CHUNK)
        far[group] = jnp.concatenate(group_rows, axis=0).T
        group_rows.clear()
        sides.append(
            remote(
                far.at[group],
                out_ref.at[:, pl.ds(pl.multiple_of(at_side + end - CHUNK, 128), CHUNK)],
                side_sem.at[0, group], side_sem.at[1, group], sib,
            )
        )
        sides[-1].start()
        out_ref[:, pl.ds(pl.multiple_of(at_out + end - CHUNK, 128), CHUNK)] = (
            factor * times_transposed(both[pl.ds(0, rows), :], other[chunk, :])
        )

    def came_back(i):
        backs[i].wait_recv()
        out_ref[parts[i], pl.ds(at_far, rows)] = far_in[parts[i], :].astype(jnp.float32)

    last = len(parts) - 1
    for copy in blocks + [beside]:
        copy.wait_send()
    for i, copy in enumerate(onward):
        pl.when(hands_on(i))(copy.wait_send)
    pl.when(lifter)(lift_on.wait_send)
    for i in range(last):
        came_back(i)
    for copy in backs[: last - 1]:
        copy.wait_send()
    for copy in sides:
        copy.wait()
    came_back(last)
    for copy in backs[last - 1 :]:
        copy.wait_send()


def shards(pair_density, table, gvec, val_energy, cond_energy):
    rows, width = pair_density.shape
    n = lax.axis_size("blk")
    nk, nv = val_energy.shape
    nc = cond_energy.shape[1]
    chunks = rows // CHUNK
    anywhere = pl.BlockSpec(memory_space=pltpu.HBM)
    return pl.pallas_call(
        functools.partial(kernel, n),
        out_shape=jax.ShapeDtypeStruct((rows, 5 * rows), jnp.float32),
        in_specs=[anywhere] * 5,
        out_specs=pl.BlockSpec(memory_space=pltpu.VMEM),
        scratch_shapes=[
            pltpu.VMEM((2 * rows, width), jnp.bfloat16),
            pltpu.VMEM((rows, width), jnp.bfloat16),
            pltpu.VMEM((rows, width), jnp.bfloat16),
            pltpu.VMEM((chunks, rows, CHUNK), jnp.float32),
            pltpu.VMEM((rows, rows), jnp.bfloat16),
            pltpu.VMEM((rows, rows), jnp.bfloat16),
            pltpu.VMEM((3, rows), jnp.int32),
            pltpu.VMEM((3, width), jnp.int32),
            pltpu.VMEM((nv, nk), jnp.float32),
            pltpu.VMEM((nc, nk), jnp.float32),
            pltpu.VMEM((48, nk), jnp.bfloat16),
            pltpu.VMEM((1, width), jnp.float32),
            pltpu.VMEM((1, rows), jnp.float32),
            pltpu.SemaphoreType.DMA((5,)),
            pltpu.SemaphoreType.DMA((2,)),
            pltpu.SemaphoreType.DMA((2, len(PIECES))),
            pltpu.SemaphoreType.DMA((2, len(PIECES))),
            pltpu.SemaphoreType.DMA((2, chunks)),
            pltpu.SemaphoreType.DMA((2, len(PIECES))),
            pltpu.SemaphoreType.REGULAR,
            pltpu.SemaphoreType.REGULAR,
            pltpu.SemaphoreType.REGULAR,
        ],
        compiler_params=pltpu.CompilerParams(
            collective_id=0, has_side_effects=True, vmem_limit_bytes=32 << 20
        ),
        name="band",
    )(*[pltpu.with_memory_space_constraint(v, pltpu.HBM) for v in (pair_density, table, gvec, val_energy.T, cond_energy.T)])


def solution(mesh):
    return jax.shard_map(
        shards,
        mesh=mesh,
        in_specs=(P("blk", None), P(None, "blk"), P(), P(), P()),
        out_specs=P("blk", None),
        check_vma=False,
    )
```
